256 devices in a mesh: vir: 32 (over x, z), occ: 4 (over y), rep: 2 (over core).
Axes of the slice: x: 4, y: 4, z: 8, core: 2. Of those that a mesh axis runs over, the one named last changes fastest.
Arguments:
- amplitudes: float32 [256, 64, 4096], P('vir', ('occ', 'rep')), may hold values from -6 to 6
- integrals: float32 [384, 512, 4096], P('vir', None, ('occ', 'rep')), may hold values from -0.005859375 to 0.005859375
- block_owner: int32 [256], replicated, may hold values from 0 to 31, as said below
Outputs:
- ladder: float32 [64, 512], P('occ', 'rep')
The draws below stay inside these ranges and needn't reach their ends.
Inputs may be any that keep to these rules, and one draw needn't show every extreme that they name: `block_owner`: blocks 8 * s to 8 * s + 7 start on vir index s. No vir index owns more than 12 blocks and some owns exactly 12; slots beyond an index's count are unused. No vir index's starting blocks name one owner more than 2 times, and each names some owner exactly 2 times.
All inputs are finite; a program needn't handle non-finite values.
Results may differ from the reference program's by a relative error of at most 0.0001.
Values sent between devices are 32-bit elements; how exact they have to be, the bound alone decides.
No kernel may reach another device: no remote copies, remote signals or barrier semaphores. Data moves between devices by JAX's collectives and lax.ppermute only.
A program may use at most 128 MiB of HBM per device.

```python
import jax
import jax.numpy as jnp
from jax import lax

VT = 64
BLK_DEV = 8
AB = 512
NPAIR = 64
NB = 256
BMAX = 12
N_VIR = 32


def draw_block_owner(key, part):
    key = jax.random.fold_in(key, 11)
    first_key, second_key = jax.random.split(key)
    source_order = jax.random.permutation(first_key, N_VIR).astype(jnp.int32)
    owner_order = jax.random.permutation(second_key, N_VIR).astype(jnp.int32)
    block_ids = jnp.arange(NB, dtype=jnp.int32)
    source_ids = block_ids // BLK_DEV
    column_ids = block_ids % BLK_DEV
    target_pos = source_order[source_ids] + column_ids
    target_pos = jnp.where(column_ids >= BLK_DEV // 2, target_pos - target_pos % 2, target_pos)
    return owner_order[target_pos % N_VIR].astype(jnp.int32)


def steps_of(rng, dims, pieces, low, top_value):
    def one(position, parts):
        steps = jax.random.uniform(jax.random.fold_in(jax.random.fold_in(rng, 6), position), (parts,), jnp.float32, low / len(pieces), top_value / len(pieces))
        return jnp.repeat(jnp.exp(steps), dims[position] // parts).reshape((-1,) + (1,) * (len(dims) - position - 1))

    level = one(*pieces[0])
    for cut in pieces[1:]:
        level = level * one(*cut)
    return level


def noise(rng, extent, scale, bound, cuts=(), kind=jnp.bfloat16):
    entries = jax.random.normal(rng, extent, jnp.float32) * scale
    if len(cuts) > 0:
        entries = steps_of(rng, extent, cuts, -0.22, 0.18) * entries
    return jnp.clip(entries, min=-bound, max=bound).astype(kind)


def setup_inputs(seed: int = 0) -> dict:
    key_list = jax.random.split(jax.random.key(seed), 4)
    return {
        "amplitudes": noise(key_list[0], (NB, NPAIR, VT * VT), 1.0, 6.0, ((0, 32), (1, 8)), jnp.float32),
        "integrals": noise(key_list[1], (N_VIR * BMAX, AB, VT * VT), (BLK_DEV * N_VIR * VT * VT) ** -0.5, 0.005859375, ((0, 32), (2, 8)), jnp.float32),
        "block_owner": draw_block_owner(jax.random.fold_in(key_list[3], 71), 0),
    }


def owner_ranks(owners):
    block_ids = jnp.arange(owners.shape[0], dtype=jnp.int32)
    earlier = block_ids[None, :] < block_ids[:, None]
    same_owner = owners[None, :] == owners[:, None]
    return jnp.sum(jnp.where(same_owner & earlier, 1, 0), axis=1).astype(jnp.int32)


def reference(amplitudes, integrals, block_owner):
    owner_rank = owner_ranks(block_owner)
    slot_index = (block_owner * BMAX + owner_rank).astype(jnp.int32)

    def ladder_step(summed, scan_item):
        amp_block, index_now = scan_item
        integral_tile = lax.dynamic_index_in_dim(integrals, index_now, 0, keepdims=False)
        term = jnp.dot(amp_block, integral_tile.T, precision=lax.Precision.HIGHEST, preferred_element_type=jnp.float32)
        return summed + term, None

    start_sum = jnp.zeros((amplitudes.shape[1], integrals.shape[1]), jnp.float32)
    ladder, _ = lax.scan(ladder_step, start_sum, (amplitudes, slot_index))
    return ladder
```

```python
import functools

import jax
import jax.numpy as jnp
from jax import lax
from jax.experimental import pallas as pl
from jax.experimental.pallas import tpu as pltpu
from jax.sharding import PartitionSpec as P

ALL = ("vir", "occ", "rep")
VIR = 32
GRP = 8
BLKS = 8
SLOTS = 12
LANE = 128
MIB = 1 << 20


def slot_of_block(owners):
    ids = jnp.arange(owners.shape[0], dtype=jnp.int32)
    earlier = ids[None, :] < ids[:, None]
    same = owners[None, :] == owners[:, None]
    rank = jnp.sum(jnp.where(same & earlier, 1, 0), axis=1).astype(jnp.int32)
    return owners * SLOTS + rank


def spread_kernel(amp_ref, out_ref):
    for blk in range(BLKS):
        for chunk in range(32):
            part, quarter = chunk // 4, chunk % 4
            out_ref[pl.ds((quarter * GRP + part) * BLKS + blk, 8, stride=4 * GRP * BLKS), :] = (
                amp_ref[pl.ds(blk * 8, 8), pl.ds(chunk * LANE, LANE)]
            )


def spread(amp):
    return pl.pallas_call(
        spread_kernel,
        out_shape=jax.ShapeDtypeStruct((VIR * GRP * BLKS, LANE), jnp.float32),
        in_specs=[pl.BlockSpec(memory_space=pltpu.VMEM)],
        out_specs=pl.BlockSpec(memory_space=pltpu.VMEM),
        compiler_params=pltpu.CompilerParams(vmem_limit_bytes=8 * MIB),
        cost_estimate=pl.CostEstimate(flops=0, bytes_accessed=2 * MIB, transcendentals=0),
        name="spread",
    )(amp)


def route_kernel(slot_ref, got_ref, out_ref):
    def clear(i, carry):
        out_ref[pl.ds(i * SLOTS, SLOTS)] = jnp.zeros((SLOTS, GRP, LANE), jnp.float32)
        return carry

    lax.fori_loop(0, VIR, clear, 0)

    for source in range(VIR):
        for blk in range(BLKS):
            out_ref[slot_ref[source * BLKS + blk]] = got_ref[
                pl.ds(source * GRP * BLKS + blk, GRP, stride=BLKS), :
            ]


def route(slot, got):
    return pl.pallas_call(
        route_kernel,
        out_shape=jax.ShapeDtypeStruct((VIR * SLOTS, GRP, LANE), jnp.float32),
        in_specs=[
            pl.BlockSpec(memory_space=pltpu.SMEM),
            pl.BlockSpec(memory_space=pltpu.VMEM),
        ],
        out_specs=pl.BlockSpec(memory_space=pltpu.VMEM),
        compiler_params=pltpu.CompilerParams(vmem_limit_bytes=8 * MIB),
        cost_estimate=pl.CostEstimate(flops=0, bytes_accessed=3 * MIB, transcendentals=0),
        name="route",
    )(slot, got)


def split(value):
    high = value.astype(jnp.bfloat16)
    return high, (value - high.astype(jnp.float32)).astype(jnp.bfloat16)


def dot_nt(left, right):
    return lax.dot_general(
        left, right, (((1,), (1,)), ((), ())), preferred_element_type=jnp.float32
    )


def contract_kernel(place_ref, amp_ref, int_ref, *refs):
    outs, (acc, tiles, ordered) = refs[:8], refs[8:]
    slot = pl.program_id(0)

    @pl.when(slot == 0)
    def _():
        acc[...] = jnp.zeros_like(acc)

    rows = jnp.concatenate(
        [amp_ref[:, q, slot].reshape(64, LANE) for q in range(4)], axis=1
    )
    a_high, a_low = split(rows)
    b_high, b_low = split(int_ref[0])
    both = dot_nt(jnp.concatenate([a_high, a_low], axis=0), b_high)
    acc[...] += both[:64] + both[64:] + dot_nt(a_high, b_low)

    @pl.when(slot == SLOTS - 1)
    def _():
        occ, rep = place_ref[0], place_ref[1]
        for tile in range(4):
            tiles[tile] = acc[:, pl.ds(tile * LANE, LANE)]
        for tile in range(4):
            for group in range(GRP):
                ordered[tile // 2, pl.ds(group * 8, 8), pl.ds(tile % 2 * LANE, LANE)] = tiles[
                    tile, pl.ds(group, 8, stride=GRP), :
                ]
        for k in range(8):
            row = lax.rem(occ + k // 2, 4) * 16
            half = rep if k % 2 == 0 else 1 - rep
            outs[k][...] = ordered[half, pl.ds(pl.multiple_of(row, 16), 16), :]


def contract(place, amp, integrals):
    piece = jax.ShapeDtypeStruct((16, 256), jnp.float32)
    return pl.pallas_call(
        contract_kernel,
        grid=(SLOTS,),
        out_shape=[piece] * 8,
        in_specs=[
            pl.BlockSpec(memory_space=pltpu.SMEM),
            pl.BlockSpec((8, 4, SLOTS, GRP, LANE), lambda i: (0, 0, 0, 0, 0)),
            pl.BlockSpec((1, 512, 512), lambda i: (i, 0, 0)),
        ],
        out_specs=[pl.BlockSpec((16, 256), lambda i: (0, 0))] * 8,
        scratch_shapes=[
            pltpu.VMEM((64, 512), jnp.float32),
            pltpu.VMEM((4, 64, LANE), jnp.float32),
            pltpu.VMEM((2, 64, 256), jnp.float32),
        ],
        compiler_params=pltpu.CompilerParams(vmem_limit_bytes=16 * MIB),
        cost_estimate=pl.CostEstimate(
            flops=6 * 64 * 512 * 6144, bytes_accessed=14 * MIB, transcendentals=0
        ),
        name="contract",
    )(place, amp, integrals)


def sum_ring_kernel(size, place_ref, *refs):
    ins, out_ref, held = refs[:size], refs[size], refs[size + 1]
    for k in range(size):
        held[lax.rem(place_ref[0] + size - k, size)] = ins[k][...]
    total = held[0]
    for k in range(1, size):
        total = total + held[k]
    out_ref[...] = total


def sum_ring(place, pieces):
    size = len(pieces)
    return pl.pallas_call(
        functools.partial(sum_ring_kernel, size),
        out_shape=jax.ShapeDtypeStruct((16, 256), jnp.float32),
        in_specs=[pl.BlockSpec(memory_space=pltpu.SMEM)]
        + [pl.BlockSpec(memory_space=pltpu.VMEM)] * size,
        out_specs=pl.BlockSpec(memory_space=pltpu.VMEM),
        scratch_shapes=[pltpu.VMEM((size, 16, 256), jnp.float32)],
        compiler_params=pltpu.CompilerParams(vmem_limit_bytes=4 * MIB),
        name="sum_ring",
    )(place, *pieces)


def group_shift(k):
    return [
        (o * 2 + r, (o + k // 2) % 4 * 2 + (r ^ (k % 2))) for o in range(4) for r in range(2)
    ]


def x_shift(k):
    return [(x * 8 + z, (x + k) % 4 * 8 + z) for x in range(4) for z in range(8)]


def z_shift(k):
    return [(x * 8 + z, x * 8 + (z + k) % 8) for x in range(4) for z in range(8)]


def on_device(amplitudes, integrals, block_owner):
    vir, occ, rep = (lax.axis_index(name) for name in ALL)
    slot = slot_of_block(block_owner)
    sent = spread(amplitudes.reshape(BLKS * 8, 4096))
    sent = sent.reshape(VIR * GRP, BLKS, LANE)
    got = lax.all_to_all(sent, ALL, split_axis=0, concat_axis=0, tiled=True)
    routed = route(slot, got.reshape(VIR * GRP * BLKS, LANE))
    owned = lax.all_to_all(
        routed.reshape(VIR, SLOTS * GRP, LANE), "vir", split_axis=0, concat_axis=0, tiled=True
    )
    pieces = contract(
        jnp.stack([occ, rep]), owned.reshape(8, 4, SLOTS, GRP, LANE), integrals
    )
    arrived = [pieces[0]] + [
        lax.ppermute(pieces[k], ("occ", "rep"), group_shift(k)) for k in range(1, 8)
    ]
    total = sum(arrived[1:], arrived[0])
    total = sum_ring(
        (vir // 8)[None],
        [total] + [lax.ppermute(total, "vir", x_shift(k)) for k in range(1, 4)],
    )
    return sum_ring(
        (vir % 8)[None],
        [total] + [lax.ppermute(total, "vir", z_shift(k)) for k in range(1, 8)],
    )


def solution(mesh):
    in_specs = (P("vir", ("occ", "rep"), None), P("vir", None, ("occ", "rep")), P())
    out_specs = P("occ", "rep")
    return jax.shard_map(
        on_device, mesh=mesh, in_specs=in_specs, out_specs=out_specs, check_vma=False
    )
```

```python
import jax
import jax.numpy as jnp
from jax import lax
from jax.experimental import pallas as pl
from jax.experimental.pallas import tpu as pltpu
from jax.sharding import PartitionSpec as P

ALL = ("vir", "occ", "rep")
VIR = 32
GRP = 8
BLKS = 8
SLOTS = 12
LANE = 128
AHEAD = 6
MIB = 1 << 20


def slot_of_block(owners):
    ids = jnp.arange(owners.shape[0], dtype=jnp.int32)
    earlier = ids[None, :] < ids[:, None]
    same = owners[None, :] == owners[:, None]
    rank = jnp.sum(jnp.where(same & earlier, 1, 0), axis=1).astype(jnp.int32)
    return owners * SLOTS + rank


def spread_kernel(amp_ref, out_ref):
    for blk in range(BLKS):
        for chunk in range(32):
            part, quarter = chunk // 4, chunk % 4
            out_ref[pl.ds((quarter * GRP + part) * BLKS + blk, 8, stride=4 * GRP * BLKS), :] = (
                amp_ref[pl.ds(blk * 8, 8), pl.ds(chunk * LANE, LANE)]
            )


def spread(amp):
    return pl.pallas_call(
        spread_kernel,
        out_shape=jax.ShapeDtypeStruct((VIR * GRP * BLKS, LANE), jnp.float32),
        in_specs=[pl.BlockSpec(memory_space=pltpu.VMEM)],
        out_specs=pl.BlockSpec(memory_space=pltpu.VMEM),
        compiler_params=pltpu.CompilerParams(vmem_limit_bytes=8 * MIB),
        cost_estimate=pl.CostEstimate(flops=0, bytes_accessed=2 * MIB, transcendentals=0),
        name="spread",
    )(amp)


def route_kernel(slot_ref, got_ref, out_ref):
    def clear(i, carry):
        out_ref[pl.ds(i * SLOTS, SLOTS)] = jnp.zeros((SLOTS, GRP, LANE), jnp.float32)
        return carry

    lax.fori_loop(0, VIR, clear, 0)

    for source in range(VIR):
        for blk in range(BLKS):
            out_ref[slot_ref[source * BLKS + blk]] = got_ref[
                pl.ds(source * GRP * BLKS + blk, GRP, stride=BLKS), :
            ]


def route(slot, got):
    return pl.pallas_call(
        route_kernel,
        out_shape=jax.ShapeDtypeStruct((VIR * SLOTS, GRP, LANE), jnp.float32),
        in_specs=[
            pl.BlockSpec(memory_space=pltpu.SMEM),
            pl.BlockSpec(memory_space=pltpu.VMEM),
        ],
        out_specs=pl.BlockSpec(memory_space=pltpu.VMEM),
        compiler_params=pltpu.CompilerParams(vmem_limit_bytes=8 * MIB),
        cost_estimate=pl.CostEstimate(flops=0, bytes_accessed=3 * MIB, transcendentals=0),
        name="route",
    )(slot, got)


def split(value):
    high = value.astype(jnp.bfloat16)
    return high, (value - high.astype(jnp.float32)).astype(jnp.bfloat16)


def dot_nt(left, right):
    return lax.dot_general(
        left, right, (((1,), (1,)), ((), ())), preferred_element_type=jnp.float32
    )


def contract_kernel(
    place_ref, amp_ref, int_hbm, other_ref, near_ref, far_ref, held, acc, tiles, ordered, sems
):
    copies = [
        pltpu.make_async_copy(int_hbm.at[slot], held.at[slot], sems.at[slot])
        for slot in range(SLOTS)
    ]
    for copy in copies[:AHEAD]:
        copy.start()
    acc[...] = jnp.zeros_like(acc)
    for slot in range(SLOTS):
        rows = jnp.concatenate(
            [amp_ref[:, q, slot].reshape(64, LANE) for q in range(4)], axis=1
        )
        a_high, a_low = split(rows)
        copies[slot].wait()
        if slot + AHEAD < SLOTS:
            copies[slot + AHEAD].start()
        b_high, b_low = split(held[slot])
        both = dot_nt(jnp.concatenate([a_high, a_low], axis=0), b_high)
        acc[...] += both[:64] + both[64:] + dot_nt(a_high, b_low)
    for tile in range(4):
        tiles[tile] = acc[:, pl.ds(tile * LANE, LANE)]
    for tile in range(4):
        for group in range(GRP):
            ordered[tile // 2, pl.ds(group * 8, 8), pl.ds(tile % 2 * LANE, LANE)] = tiles[
                tile, pl.ds(group, 8, stride=GRP), :
            ]
    occ, rep = place_ref[0], place_ref[1]
    for k in range(4):
        rows = pl.ds(pl.multiple_of((occ ^ k) * 16, 16), 16)
        other_ref[pl.ds(k * 16, 16)] = ordered[1 - rep, rows, :]
        mine = far_ref if k >= 2 else near_ref
        mine[pl.ds(k % 2 * 16, 16)] = ordered[rep, rows, :]


def contract(place, amp, integrals):
    return pl.pallas_call(
        contract_kernel,
        out_shape=[
            jax.ShapeDtypeStruct((64, 256), jnp.float32),
            jax.ShapeDtypeStruct((32, 256), jnp.float32),
            jax.ShapeDtypeStruct((32, 256), jnp.float32),
        ],
        in_specs=[
            pl.BlockSpec(memory_space=pltpu.SMEM),
            pl.BlockSpec(memory_space=pltpu.VMEM),
            pl.BlockSpec(memory_space=pltpu.HBM),
        ],
        out_specs=[pl.BlockSpec(memory_space=pltpu.VMEM)] * 3,
        scratch_shapes=[
            pltpu.VMEM((SLOTS, 512, 512), jnp.float32),
            pltpu.VMEM((64, 512), jnp.float32),
            pltpu.VMEM((4, 64, LANE), jnp.float32),
            pltpu.VMEM((2, 64, 256), jnp.float32),
            pltpu.SemaphoreType.DMA((SLOTS,)),
        ],
        compiler_params=pltpu.CompilerParams(vmem_limit_bytes=56 * MIB),
        cost_estimate=pl.CostEstimate(
            flops=6 * 64 * 512 * 6144, bytes_accessed=14 * MIB, transcendentals=0
        ),
        name="contract",
    )(place, amp, integrals)


def flip(size, bit):
    return [(i, i ^ bit) for i in range(size)]


def on_device(amplitudes, integrals, block_owner):
    occ, rep = lax.axis_index("occ"), lax.axis_index("rep")
    slot = slot_of_block(block_owner)
    sent = spread(amplitudes.reshape(BLKS * 8, 4096))
    sent = sent.reshape(VIR * GRP, BLKS, LANE)
    got = lax.all_to_all(sent, ALL, split_axis=0, concat_axis=0, tiled=True)
    routed = route(slot, got.reshape(VIR * GRP * BLKS, LANE))
    owned = lax.all_to_all(
        routed.reshape(VIR, SLOTS * GRP, LANE), "vir", split_axis=0, concat_axis=0, tiled=True
    )
    other, near, far = contract(
        jnp.stack([occ, rep]), owned.reshape(8, 4, SLOTS, GRP, LANE), integrals
    )
    arrived = lax.ppermute(other, "rep", flip(2, 1))
    far = far + arrived[32:]
    near = near + arrived[:32]
    near = near + lax.ppermute(far, "occ", flip(4, 2))
    total = near[:16] + lax.ppermute(near[16:], "occ", flip(4, 1))
    for bit in (16, 8, 4, 2, 1):
        total = total + lax.ppermute(total, "vir", flip(VIR, bit))
    return total


def solution(mesh):
    in_specs = (P("vir", ("occ", "rep"), None), P("vir", None, ("occ", "rep")), P())
    out_specs = P("occ", "rep")
    return jax.shard_map(
        on_device, mesh=mesh, in_specs=in_specs, out_specs=out_specs, check_vma=False
    )
```

```python
import jax
import jax.numpy as jnp
from jax import lax
from jax.experimental import pallas as pl
from jax.experimental.pallas import tpu as pltpu
from jax.sharding import PartitionSpec as P

ALL = ("vir", "occ", "rep")
VIR = 32
GRP = 8
BLKS = 8
SLOTS = 12
LANE = 128
AHEAD = 6
MIB = 1 << 20


def slot_of_block(owners):
    ids = jnp.arange(owners.shape[0], dtype=jnp.int32)
    earlier = ids[None, :] < ids[:, None]
    same = owners[None, :] == owners[:, None]
    rank = jnp.sum(jnp.where(same & earlier, 1, 0), axis=1).astype(jnp.int32)
    return owners * SLOTS + rank


def spread_kernel(amp_ref, out_ref):
    for blk in range(BLKS):
        for chunk in range(32):
            part, quarter = chunk // 4, chunk % 4
            out_ref[pl.ds((quarter * GRP + part) * BLKS + blk, 8, stride=4 * GRP * BLKS), :] = (
                amp_ref[pl.ds(blk * 8, 8), pl.ds(chunk * LANE, LANE)]
            )


def spread(amp):
    return pl.pallas_call(
        spread_kernel,
        out_shape=jax.ShapeDtypeStruct((VIR * GRP * BLKS, LANE), jnp.float32),
        in_specs=[pl.BlockSpec(memory_space=pltpu.VMEM)],
        out_specs=pl.BlockSpec(memory_space=pltpu.VMEM),
        compiler_params=pltpu.CompilerParams(vmem_limit_bytes=8 * MIB),
        cost_estimate=pl.CostEstimate(flops=0, bytes_accessed=2 * MIB, transcendentals=0),
        name="spread",
    )(amp)


def route_kernel(slot_ref, got_ref, out_ref):
    def clear(i, carry):
        out_ref[pl.ds(i * SLOTS, SLOTS)] = jnp.zeros((SLOTS, GRP, LANE), jnp.float32)
        return carry

    lax.fori_loop(0, VIR, clear, 0)

    for source in range(VIR):
        for blk in range(BLKS):
            out_ref[slot_ref[source * BLKS + blk]] = got_ref[
                pl.ds(source * GRP * BLKS + blk, GRP, stride=BLKS), :
            ]


def route(slot, got):
    return pl.pallas_call(
        route_kernel,
        out_shape=jax.ShapeDtypeStruct((VIR * SLOTS, GRP, LANE), jnp.float32),
        in_specs=[
            pl.BlockSpec(memory_space=pltpu.SMEM),
            pl.BlockSpec(memory_space=pltpu.VMEM),
        ],
        out_specs=pl.BlockSpec(memory_space=pltpu.VMEM),
        compiler_params=pltpu.CompilerParams(vmem_limit_bytes=8 * MIB),
        cost_estimate=pl.CostEstimate(flops=0, bytes_accessed=3 * MIB, transcendentals=0),
        name="route",
    )(slot, got)


def split(value):
    high = value.astype(jnp.bfloat16)
    return high, (value - high.astype(jnp.float32)).astype(jnp.bfloat16)


def dot_nt(left, right):
    return lax.dot_general(
        left, right, (((1,), (1,)), ((), ())), preferred_element_type=jnp.float32
    )


def contract_kernel(amp_ref, int_hbm, out_ref, held, acc, tiles, ordered, sems):
    copies = [
        pltpu.make_async_copy(int_hbm.at[slot], held.at[slot], sems.at[slot])
        for slot in range(SLOTS)
    ]
    for copy in copies[:AHEAD]:
        copy.start()
    acc[...] = jnp.zeros_like(acc)
    for slot in range(SLOTS):
        rows = jnp.concatenate(
            [amp_ref[:, q, slot].reshape(64, LANE) for q in range(4)], axis=1
        )
        a_high, a_low = split(rows)
        copies[slot].wait()
        if slot + AHEAD < SLOTS:
            copies[slot + AHEAD].start()
        b_high, b_low = split(held[slot])
        both = dot_nt(jnp.concatenate([a_high, a_low], axis=0), b_high)
        acc[...] += both[:64] + both[64:] + dot_nt(a_high, b_low)
    for tile in range(4):
        tiles[tile] = acc[:, pl.ds(tile * LANE, LANE)]
    for tile in range(4):
        for group in range(GRP):
            ordered[tile // 2, pl.ds(group * 8, 8), pl.ds(tile % 2 * LANE, LANE)] = tiles[
                tile, pl.ds(group, 8, stride=GRP), :
            ]
    for part in range(GRP):
        out_ref[part] = ordered[part % 2, pl.ds(part // 2 * 16, 16), :]


def contract(amp, integrals):
    return pl.pallas_call(
        contract_kernel,
        out_shape=jax.ShapeDtypeStruct((GRP, 16, 256), jnp.float32),
        in_specs=[
            pl.BlockSpec(memory_space=pltpu.VMEM),
            pl.BlockSpec(memory_space=pltpu.HBM),
        ],
        out_specs=pl.BlockSpec(memory_space=pltpu.VMEM),
        scratch_shapes=[
            pltpu.VMEM((SLOTS, 512, 512), jnp.float32),
            pltpu.VMEM((64, 512), jnp.float32),
            pltpu.VMEM((4, 64, LANE), jnp.float32),
            pltpu.VMEM((2, 64, 256), jnp.float32),
            pltpu.SemaphoreType.DMA((SLOTS,)),
        ],
        compiler_params=pltpu.CompilerParams(vmem_limit_bytes=50 * MIB),
        cost_estimate=pl.CostEstimate(
            flops=6 * 64 * 512 * 6144, bytes_accessed=14 * MIB, transcendentals=0
        ),
        name="contract",
    )(amp, integrals)


def sum_x_kernel(place_ref, *refs):
    ins, out_ref, held = refs[:4], refs[4], refs[5]
    for k in range(4):
        held[lax.rem(place_ref[0] + 4 - k, 4)] = ins[k][...]
    out_ref[...] = (held[0] + held[1]) + (held[2] + held[3])


def sum_x(place, pieces):
    return pl.pallas_call(
        sum_x_kernel,
        out_shape=jax.ShapeDtypeStruct((16, 256), jnp.float32),
        in_specs=[pl.BlockSpec(memory_space=pltpu.SMEM)]
        + [pl.BlockSpec(memory_space=pltpu.VMEM)] * 4,
        out_specs=pl.BlockSpec(memory_space=pltpu.VMEM),
        scratch_shapes=[pltpu.VMEM((4, 16, 256), jnp.float32)],
        compiler_params=pltpu.CompilerParams(vmem_limit_bytes=4 * MIB),
        name="sum_x",
    )(place, *pieces)


def x_shift(k):
    return [(x * 8 + z, (x + k) % 4 * 8 + z) for x in range(4) for z in range(8)]


def on_device(amplitudes, integrals, block_owner):
    x_place = (lax.axis_index("vir") // 8)[None]
    slot = slot_of_block(block_owner)
    sent = spread(amplitudes.reshape(BLKS * 8, 4096))
    sent = sent.reshape(VIR * GRP, BLKS, LANE)
    got = lax.all_to_all(sent, ALL, split_axis=0, concat_axis=0, tiled=True)
    routed = route(slot, got.reshape(VIR * GRP * BLKS, LANE))
    owned = lax.all_to_all(
        routed.reshape(VIR, SLOTS * GRP, LANE), "vir", split_axis=0, concat_axis=0, tiled=True
    )
    pieces = contract(owned.reshape(8, 4, SLOTS, GRP, LANE), integrals)
    total = jnp.sum(lax.all_to_all(pieces, ("occ", "rep"), 0, 0, tiled=True), axis=0)
    total = sum_x(
        x_place, [total] + [lax.ppermute(total, "vir", x_shift(k)) for k in range(1, 4)]
    )
    every_z = [[x * 8 + z for z in range(8)] for x in range(4)]
    copies = jnp.broadcast_to(total[None], (8, 16, 256))
    return jnp.sum(
        lax.all_to_all(copies, "vir", 0, 0, axis_index_groups=every_z, tiled=True), axis=0
    )


def solution(mesh):
    in_specs = (P("vir", ("occ", "rep"), None), P("vir", None, ("occ", "rep")), P())
    out_specs = P("occ", "rep")
    return jax.shard_map(
        on_device, mesh=mesh, in_specs=in_specs, out_specs=out_specs, check_vma=False
    )
```

```python
import jax
import jax.numpy as jnp
from jax import lax
from jax.experimental import pallas as pl
from jax.experimental.pallas import tpu as pltpu
from jax.sharding import Mesh
from jax.sharding import PartitionSpec as P

VIR = 32
GRP = 8
BLKS = 8
SLOTS = 12
LANE = 128
AHEAD = 6
MIB = 1 << 20


def slot_of_block(owners):
    ids = jnp.arange(owners.shape[0], dtype=jnp.int32)
    earlier = ids[None, :] < ids[:, None]
    same = owners[None, :] == owners[:, None]
    rank = jnp.sum(jnp.where(same & earlier, 1, 0), axis=1).astype(jnp.int32)
    return (owners % 8 * 4 + owners // 8) * SLOTS + rank


def spread_kernel(amp_ref, out_ref):
    for blk in range(BLKS):
        for chunk in range(32):
            part, quarter = chunk // 4, chunk % 4
            first = (part * VIR + quarter) * BLKS + blk
            out_ref[pl.ds(first, 8, stride=4 * BLKS), :] = amp_ref[
                pl.ds(blk * 8, 8), pl.ds(chunk * LANE, LANE)
            ]


def spread(amp):
    return pl.pallas_call(
        spread_kernel,
        out_shape=jax.ShapeDtypeStruct((VIR * GRP * BLKS, LANE), jnp.float32),
        in_specs=[pl.BlockSpec(memory_space=pltpu.VMEM)],
        out_specs=pl.BlockSpec(memory_space=pltpu.VMEM),
        compiler_params=pltpu.CompilerParams(vmem_limit_bytes=8 * MIB),
        cost_estimate=pl.CostEstimate(flops=0, bytes_accessed=2 * MIB, transcendentals=0),
        name="spread",
    )(amp)


def route_kernel(slot_ref, got_ref, out_ref):
    def clear(i, carry):
        out_ref[pl.ds(i * SLOTS, SLOTS)] = jnp.zeros((SLOTS, GRP, LANE), jnp.float32)
        return carry

    lax.fori_loop(0, VIR, clear, 0)

    for source in range(VIR):
        for blk in range(BLKS):
            vir = source % 4 * 8 + source // 4
            out_ref[slot_ref[vir * BLKS + blk]] = got_ref[
                pl.ds(source * BLKS + blk, GRP, stride=VIR * BLKS), :
            ]


def route(slot, got):
    return pl.pallas_call(
        route_kernel,
        out_shape=jax.ShapeDtypeStruct((VIR * SLOTS, GRP, LANE), jnp.float32),
        in_specs=[
            pl.BlockSpec(memory_space=pltpu.SMEM),
            pl.BlockSpec(memory_space=pltpu.VMEM),
        ],
        out_specs=pl.BlockSpec(memory_space=pltpu.VMEM),
        compiler_params=pltpu.CompilerParams(vmem_limit_bytes=8 * MIB),
        cost_estimate=pl.CostEstimate(flops=0, bytes_accessed=3 * MIB, transcendentals=0),
        name="route",
    )(slot, got)


def split(value):
    high = value.astype(jnp.bfloat16)
    return high, (value - high.astype(jnp.float32)).astype(jnp.bfloat16)


def dot_nt(left, right):
    return lax.dot_general(
        left, right, (((1,), (1,)), ((), ())), preferred_element_type=jnp.float32
    )


def contract_kernel(amp_ref, int_hbm, out_ref, held, acc, tiles, ordered, sems):
    copies = [
        pltpu.make_async_copy(int_hbm.at[slot], held.at[slot], sems.at[slot])
        for slot in range(SLOTS)
    ]
    for copy in copies[:AHEAD]:
        copy.start()
    acc[...] = jnp.zeros_like(acc)
    for slot in range(SLOTS):
        rows = jnp.concatenate(
            [amp_ref[:, q, slot].reshape(64, LANE) for q in range(4)], axis=1
        )
        a_high, a_low = split(rows)
        copies[slot].wait()
        if slot + AHEAD < SLOTS:
            copies[slot + AHEAD].start()
        b_high, b_low = split(held[slot])
        both = dot_nt(jnp.concatenate([a_high, a_low], axis=0), b_high)
        acc[...] += both[:64] + both[64:] + dot_nt(a_high, b_low)
    for tile in range(4):
        tiles[tile] = acc[:, pl.ds(tile * LANE, LANE)]
    for tile in range(4):
        for group in range(GRP):
            ordered[tile // 2, pl.ds(group * 8, 8), pl.ds(tile % 2 * LANE, LANE)] = tiles[
                tile, pl.ds(group, 8, stride=GRP), :
            ]
    for part in range(GRP):
        out_ref[part] = ordered[part % 2, pl.ds(part // 2 * 16, 16), :]


def contract(amp, integrals):
    return pl.pallas_call(
        contract_kernel,
        out_shape=jax.ShapeDtypeStruct((GRP, 16, 256), jnp.float32),
        in_specs=[
            pl.BlockSpec(memory_space=pltpu.VMEM),
            pl.BlockSpec(memory_space=pltpu.HBM),
        ],
        out_specs=pl.BlockSpec(memory_space=pltpu.VMEM),
        scratch_shapes=[
            pltpu.VMEM((SLOTS, 512, 512), jnp.float32),
            pltpu.VMEM((64, 512), jnp.float32),
            pltpu.VMEM((4, 64, LANE), jnp.float32),
            pltpu.VMEM((2, 64, 256), jnp.float32),
            pltpu.SemaphoreType.DMA((SLOTS,)),
        ],
        compiler_params=pltpu.CompilerParams(vmem_limit_bytes=50 * MIB),
        cost_estimate=pl.CostEstimate(
            flops=6 * 64 * 512 * 6144, bytes_accessed=14 * MIB, transcendentals=0
        ),
        name="contract",
    )(amp, integrals)


def sum_x_kernel(place_ref, *refs):
    ins, out_ref, held = refs[:4], refs[4], refs[5]
    for k in range(4):
        held[lax.rem(place_ref[0] + 4 - k, 4)] = ins[k][...]
    out_ref[...] = (held[0] + held[1]) + (held[2] + held[3])


def sum_x(place, pieces):
    return pl.pallas_call(
        sum_x_kernel,
        out_shape=jax.ShapeDtypeStruct((16, 256), jnp.float32),
        in_specs=[pl.BlockSpec(memory_space=pltpu.SMEM)]
        + [pl.BlockSpec(memory_space=pltpu.VMEM)] * 4,
        out_specs=pl.BlockSpec(memory_space=pltpu.VMEM),
        scratch_shapes=[pltpu.VMEM((4, 16, 256), jnp.float32)],
        compiler_params=pltpu.CompilerParams(vmem_limit_bytes=4 * MIB),
        name="sum_x",
    )(place, *pieces)


def x_shift(k):
    return [(x, (x + k) % 4) for x in range(4)]


def on_device(amplitudes, integrals, block_owner):
    x_place = lax.axis_index("x")[None]
    slot = slot_of_block(block_owner)
    sent = spread(amplitudes.reshape(BLKS * 8, 4096))
    sent = sent.reshape(VIR * GRP, BLKS, LANE)
    got = lax.all_to_all(sent, ("occ", "rep", "z", "x"), 0, 0, tiled=True)
    routed = route(slot, got.reshape(VIR * GRP * BLKS, LANE))
    owned = lax.all_to_all(routed.reshape(VIR, SLOTS * GRP, LANE), ("z", "x"), 0, 0, tiled=True)
    pieces = contract(owned.reshape(8, 4, SLOTS, GRP, LANE), integrals)
    total = jnp.sum(lax.all_to_all(pieces, ("occ", "rep"), 0, 0, tiled=True), axis=0)
    total = sum_x(
        x_place, [total] + [lax.ppermute(total, "x", x_shift(k)) for k in range(1, 4)]
    )
    copies = jnp.broadcast_to(total[None], (8, 16, 256))
    return jnp.sum(lax.all_to_all(copies, "z", 0, 0, tiled=True), axis=0)


def solution(mesh):
    grid = Mesh(mesh.devices.reshape(4, 8, 4, 2), ("x", "z", "occ", "rep"))
    vir, group = ("x", "z"), ("occ", "rep")
    return jax.shard_map(
        on_device,
        mesh=grid,
        in_specs=(P(vir, group, None), P(vir, None, group), P()),
        out_specs=P("occ", "rep"),
        check_vma=False,
    )
```

```python
import jax
import jax.numpy as jnp
from jax import lax
from jax.experimental import pallas as pl
from jax.experimental.pallas import tpu as pltpu
from jax.sharding import Mesh
from jax.sharding import PartitionSpec as P

VIR = 32
GRP = 8
BLKS = 8
SLOTS = 12
LANE = 128
AHEAD = 6
MIB = 1 << 20


def slot_of_block(owners):
    ids = jnp.arange(owners.shape[0], dtype=jnp.int32)
    earlier = ids[None, :] < ids[:, None]
    same = owners[None, :] == owners[:, None]
    rank = jnp.sum(jnp.where(same & earlier, 1, 0), axis=1).astype(jnp.int32)
    return (owners % 8 * 4 + owners // 8) * SLOTS + rank


def spread_kernel(amp_hbm, out_hbm, amp, out, in_sems, out_sems):
    wide, rows = 4 * LANE, VIR * BLKS
    arrive = [
        pltpu.make_async_copy(
            amp_hbm.at[:, pl.ds(part * wide, wide)], amp.at[part], in_sems.at[part]
        )
        for part in range(GRP)
    ]
    leave = [
        pltpu.make_async_copy(
            out.at[part], out_hbm.at[pl.ds(part * rows, rows)], out_sems.at[part]
        )
        for part in range(GRP)
    ]
    for copy in arrive:
        copy.start()
    for part in range(GRP):
        arrive[part].wait()
        for blk in range(BLKS):
            for quarter in range(4):
                out[part, pl.ds(quarter * BLKS + blk, 8, stride=4 * BLKS), :] = amp[
                    part, pl.ds(blk * 8, 8), pl.ds(quarter * LANE, LANE)
                ]
        leave[part].start()
    for copy in leave:
        copy.wait()


def spread(amp):
    return pl.pallas_call(
        spread_kernel,
        out_shape=jax.ShapeDtypeStruct((VIR * GRP * BLKS, LANE), jnp.float32),
        in_specs=[pl.BlockSpec(memory_space=pltpu.HBM)],
        out_specs=pl.BlockSpec(memory_space=pltpu.HBM),
        scratch_shapes=[
            pltpu.VMEM((GRP, BLKS * 8, 4 * LANE), jnp.float32),
            pltpu.VMEM((GRP, VIR * BLKS, LANE), jnp.float32),
            pltpu.SemaphoreType.DMA((GRP,)),
            pltpu.SemaphoreType.DMA((GRP,)),
        ],
        compiler_params=pltpu.CompilerParams(vmem_limit_bytes=60 * MIB),
        cost_estimate=pl.CostEstimate(flops=0, bytes_accessed=2 * MIB, transcendentals=0),
        name="spread",
    )(amp)


def route_kernel(slot_ref, got_ref, out_ref):
    def clear(i, carry):
        out_ref[pl.ds(i * SLOTS, SLOTS)] = jnp.zeros((SLOTS, GRP, LANE), jnp.float32)
        return carry

    lax.fori_loop(0, VIR, clear, 0)

    for source in range(VIR):
        for blk in range(BLKS):
            vir = source % 4 * 8 + source // 4
            out_ref[slot_ref[vir * BLKS + blk]] = got_ref[
                pl.ds(source * BLKS + blk, GRP, stride=VIR * BLKS), :
            ]


def route(slot, got):
    return pl.pallas_call(
        route_kernel,
        out_shape=jax.ShapeDtypeStruct((VIR * SLOTS, GRP, LANE), jnp.float32),
        in_specs=[
            pl.BlockSpec(memory_space=pltpu.SMEM),
            pl.BlockSpec(memory_space=pltpu.VMEM),
        ],
        out_specs=pl.BlockSpec(memory_space=pltpu.VMEM),
        compiler_params=pltpu.CompilerParams(vmem_limit_bytes=8 * MIB),
        cost_estimate=pl.CostEstimate(flops=0, bytes_accessed=3 * MIB, transcendentals=0),
        name="route",
    )(slot, got)


def split(value):
    high = value.astype(jnp.bfloat16)
    return high, (value - high.astype(jnp.float32)).astype(jnp.bfloat16)


def dot_nt(left, right):
    return lax.dot_general(
        left, right, (((1,), (1,)), ((), ())), preferred_element_type=jnp.float32
    )


def contract_kernel(amp_ref, int_hbm, out_ref, held, acc, tiles, sems):
    copies = [
        pltpu.make_async_copy(int_hbm.at[slot], held.at[slot], sems.at[slot])
        for slot in range(SLOTS)
    ]
    for copy in copies[:AHEAD]:
        copy.start()
    acc[...] = jnp.zeros_like(acc)
    for slot in range(SLOTS):
        rows = jnp.concatenate(
            [amp_ref[:, q, slot].reshape(64, LANE) for q in range(4)], axis=1
        )
        a_high, a_low = split(rows)
        copies[slot].wait()
        if slot + AHEAD < SLOTS:
            copies[slot + AHEAD].start()
        b_high, b_low = split(held[slot])
        both = dot_nt(jnp.concatenate([a_high, a_low], axis=0), b_high)
        acc[...] += both[:64] + both[64:] + dot_nt(a_high, b_low)
    for tile in range(4):
        tiles[tile] = acc[:, pl.ds(tile * LANE, LANE)]
    for piece in range(VIR):
        rep, occ, x = piece // 16, piece // 4 % 4, piece % 4
        out_ref[piece] = tiles[rep * 2 + x % 2, pl.ds(occ * 2 + x // 2, 8, stride=GRP), :]


def contract(amp, integrals):
    return pl.pallas_call(
        contract_kernel,
        out_shape=jax.ShapeDtypeStruct((VIR, 8, LANE), jnp.float32),
        in_specs=[
            pl.BlockSpec(memory_space=pltpu.VMEM),
            pl.BlockSpec(memory_space=pltpu.HBM),
        ],
        out_specs=pl.BlockSpec(memory_space=pltpu.VMEM),
        scratch_shapes=[
            pltpu.VMEM((SLOTS, 512, 512), jnp.float32),
            pltpu.VMEM((64, 512), jnp.float32),
            pltpu.VMEM((4, 64, LANE), jnp.float32),
            pltpu.SemaphoreType.DMA((SLOTS,)),
        ],
        compiler_params=pltpu.CompilerParams(vmem_limit_bytes=50 * MIB),
        cost_estimate=pl.CostEstimate(
            flops=6 * 64 * 512 * 6144, bytes_accessed=14 * MIB, transcendentals=0
        ),
        name="contract",
    )(amp, integrals)


def add_up_kernel(got_ref, out_ref):
    total = got_ref[0]
    for i in range(1, VIR):
        total = total + got_ref[i]
    for i in range(VIR):
        out_ref[i] = total


def finish_kernel(got_ref, out_ref):
    for x in range(4):
        total = got_ref[x]
        for z in range(1, 8):
            total = total + got_ref[z * 4 + x]
        out_ref[pl.ds(x // 2 * 8, 8), pl.ds(x % 2 * LANE, LANE)] = total


def small(kernel, got, shape):
    return pl.pallas_call(
        kernel,
        out_shape=jax.ShapeDtypeStruct(shape, jnp.float32),
        in_specs=[pl.BlockSpec(memory_space=pltpu.VMEM)],
        out_specs=pl.BlockSpec(memory_space=pltpu.VMEM),
        compiler_params=pltpu.CompilerParams(vmem_limit_bytes=4 * MIB),
        name=kernel.__name__,
    )(got)


def on_device(amplitudes, integrals, block_owner):
    slot = slot_of_block(block_owner)
    sent = spread(amplitudes.reshape(BLKS * 8, 4096))
    sent = sent.reshape(VIR * GRP, BLKS, LANE)
    got = lax.all_to_all(sent, ("occ", "rep", "z", "x"), 0, 0, tiled=True)
    routed = route(slot, got.reshape(VIR * GRP * BLKS, LANE))
    owned = lax.all_to_all(routed.reshape(VIR, SLOTS * GRP, LANE), ("z", "x"), 0, 0, tiled=True)
    pieces = contract(owned.reshape(8, 4, SLOTS, GRP, LANE), integrals)
    parts = lax.all_to_all(pieces, ("rep", "occ", "x"), 0, 0, tiled=True)
    copies = small(add_up_kernel, parts, (VIR, 8, LANE))
    parts = lax.all_to_all(copies, ("z", "x"), 0, 0, tiled=True)
    return small(finish_kernel, parts, (16, 256))


def solution(mesh):
    grid = Mesh(mesh.devices.reshape(4, 8, 4, 2), ("x", "z", "occ", "rep"))
    vir, group = ("x", "z"), ("occ", "rep")
    return jax.shard_map(
        on_device,
        mesh=grid,
        in_specs=(P(vir, group, None), P(vir, None, group), P()),
        out_specs=P("occ", "rep"),
        check_vma=False,
    )
```

```python
import jax
import jax.numpy as jnp
from jax import lax
from jax.experimental import pallas as pl
from jax.experimental.pallas import tpu as pltpu
from jax.sharding import Mesh
from jax.sharding import PartitionSpec as P

VIR = 32
GRP = 8
BLKS = 8
SLOTS = 12
LANE = 128
AHEAD = 12
MIB = 1 << 20


def spread_kernel(owner_hbm, amp_hbm, slot_ref, out_ref, owner_ref, amp, sems):
    wide = 4 * LANE
    copies = [
        pltpu.make_async_copy(
            amp_hbm.at[:, pl.ds(part * wide, wide)], amp.at[part], sems.at[part]
        )
        for part in range(GRP)
    ]
    owner_copy = pltpu.make_async_copy(owner_hbm, owner_ref, sems.at[GRP])
    owner_copy.start()
    for copy in copies:
        copy.start()

    owner_copy.wait()
    count = owner_ref.shape[1]
    owners = owner_ref[...]
    along = jnp.broadcast_to(owners.astype(jnp.float32), (count, count))
    down = along.T
    rows = lax.broadcasted_iota(jnp.int32, (count, count), 0)
    lanes = lax.broadcasted_iota(jnp.int32, (count, count), 1)
    earlier = jnp.where((down == along) & (rows < lanes), 1, 0)
    rank = jnp.sum(earlier, axis=0, keepdims=True)
    place = lax.rem(owners, 8) * 4 + lax.div(owners, 8)
    slot_ref[...] = place * SLOTS + rank

    for part in range(GRP):
        copies[part].wait()
        for blk in range(BLKS):
            for quarter in range(4):
                first = (part * VIR + quarter) * BLKS + blk
                out_ref[pl.ds(first, 8, stride=4 * BLKS), :] = amp[
                    part, pl.ds(blk * 8, 8), pl.ds(quarter * LANE, LANE)
                ]


def spread(owners, amp):
    return pl.pallas_call(
        spread_kernel,
        out_shape=[
            jax.ShapeDtypeStruct(owners.shape, jnp.int32),
            jax.ShapeDtypeStruct((VIR * GRP * BLKS, LANE), jnp.float32),
        ],
        in_specs=[pl.BlockSpec(memory_space=pltpu.HBM)] * 2,
        out_specs=[pl.BlockSpec(memory_space=pltpu.VMEM)] * 2,
        scratch_shapes=[
            pltpu.VMEM(owners.shape, jnp.int32),
            pltpu.VMEM((GRP, BLKS * 8, 4 * LANE), jnp.float32),
            pltpu.SemaphoreType.DMA((GRP + 1,)),
        ],
        compiler_params=pltpu.CompilerParams(vmem_limit_bytes=52 * MIB),
        cost_estimate=pl.CostEstimate(flops=0, bytes_accessed=2 * MIB, transcendentals=0),
        name="spread",
    )(owners, amp)


def route_kernel(slot_ref, got_ref, out_ref):
    def clear(i, carry):
        out_ref[pl.ds(i * SLOTS, SLOTS)] = jnp.zeros((SLOTS, GRP, LANE), jnp.float32)
        return carry

    lax.fori_loop(0, VIR, clear, 0)

    for source in range(VIR):
        for blk in range(BLKS):
            vir = source % 4 * 8 + source // 4
            out_ref[slot_ref[0, vir * BLKS + blk]] = got_ref[
                pl.ds(source * BLKS + blk, GRP, stride=VIR * BLKS), :
            ]


def route(slot, got):
    return pl.pallas_call(
        route_kernel,
        out_shape=jax.ShapeDtypeStruct((VIR * SLOTS, GRP, LANE), jnp.float32),
        in_specs=[
            pl.BlockSpec(memory_space=pltpu.SMEM),
            pl.BlockSpec(memory_space=pltpu.VMEM),
        ],
        out_specs=pl.BlockSpec(memory_space=pltpu.VMEM),
        compiler_params=pltpu.CompilerParams(vmem_limit_bytes=8 * MIB),
        cost_estimate=pl.CostEstimate(flops=0, bytes_accessed=3 * MIB, transcendentals=0),
        name="route",
    )(slot, got)


def split(value):
    high = value.astype(jnp.bfloat16)
    return high, (value - high.astype(jnp.float32)).astype(jnp.bfloat16)


def dot_nt(left, right):
    return lax.dot_general(
        left, right, (((1,), (1,)), ((), ())), preferred_element_type=jnp.float32
    )


def contract_kernel(amp_ref, int_hbm, out_ref, held, pair, acc, tiles, sems):
    copies = [
        pltpu.make_async_copy(int_hbm.at[slot], held.at[slot], sems.at[slot])
        for slot in range(SLOTS)
    ]
    for copy in copies[:AHEAD]:
        copy.start()
    acc[...] = jnp.zeros_like(acc)
    for slot in range(SLOTS):
        rows = jnp.concatenate(
            [amp_ref[:, q, slot].reshape(64, LANE) for q in range(4)], axis=1
        )
        pair[slot] = jnp.concatenate(split(rows), axis=0)
    for slot in range(SLOTS):
        copies[slot].wait()
        if slot + AHEAD < SLOTS:
            copies[slot + AHEAD].start()
        b_high, b_low = split(held[slot])
        both = dot_nt(pair[slot], b_high)
        acc[...] += both[:64] + both[64:] + dot_nt(pair[slot, :64], b_low)
    for tile in range(4):
        tiles[tile] = acc[:, pl.ds(tile * LANE, LANE)]
    for piece in range(VIR):
        rep, occ, x = piece // 16, piece // 4 % 4, piece % 4
        out_ref[piece] = tiles[rep * 2 + x % 2, pl.ds(occ * 2 + x // 2, 8, stride=GRP), :]


def contract(amp, integrals):
    return pl.pallas_call(
        contract_kernel,
        out_shape=jax.ShapeDtypeStruct((VIR, 8, LANE), jnp.float32),
        in_specs=[
            pl.BlockSpec(memory_space=pltpu.VMEM),
            pl.BlockSpec(memory_space=pltpu.HBM),
        ],
        out_specs=pl.BlockSpec(memory_space=pltpu.VMEM),
        scratch_shapes=[
            pltpu.VMEM((SLOTS, 512, 512), jnp.float32),
            pltpu.VMEM((SLOTS, 128, 512), jnp.bfloat16),
            pltpu.VMEM((64, 512), jnp.float32),
            pltpu.VMEM((4, 64, LANE), jnp.float32),
            pltpu.SemaphoreType.DMA((SLOTS,)),
        ],
        compiler_params=pltpu.CompilerParams(vmem_limit_bytes=50 * MIB),
        cost_estimate=pl.CostEstimate(
            flops=6 * 64 * 512 * 6144, bytes_accessed=14 * MIB, transcendentals=0
        ),
        name="contract",
    )(amp, integrals)


def add_up_kernel(got_ref, out_ref):
    total = got_ref[0]
    for i in range(1, VIR):
        total = total + got_ref[i]
    for i in range(VIR):
        out_ref[i] = total


def finish_kernel(got_ref, out_ref):
    for x in range(4):
        total = got_ref[x]
        for z in range(1, 8):
            total = total + got_ref[z * 4 + x]
        out_ref[pl.ds(x // 2 * 8, 8), pl.ds(x % 2 * LANE, LANE)] = total


def small(kernel, got, shape):
    return pl.pallas_call(
        kernel,
        out_shape=jax.ShapeDtypeStruct(shape, jnp.float32),
        in_specs=[pl.BlockSpec(memory_space=pltpu.VMEM)],
        out_specs=pl.BlockSpec(memory_space=pltpu.VMEM),
        compiler_params=pltpu.CompilerParams(vmem_limit_bytes=4 * MIB),
        name=kernel.__name__,
    )(got)


def on_device(amplitudes, integrals, block_owner):
    slot, sent = spread(block_owner.reshape(1, -1), amplitudes.reshape(BLKS * 8, 4096))
    sent = sent.reshape(VIR * GRP, BLKS, LANE)
    got = lax.all_to_all(sent, ("occ", "rep", "z", "x"), 0, 0, tiled=True)
    routed = route(slot, got.reshape(VIR * GRP * BLKS, LANE))
    owned = lax.all_to_all(routed.reshape(VIR, SLOTS * GRP, LANE), ("z", "x"), 0, 0, tiled=True)
    pieces = contract(owned.reshape(8, 4, SLOTS, GRP, LANE), integrals)
    parts = lax.all_to_all(pieces, ("rep", "occ", "x"), 0, 0, tiled=True)
    copies = small(add_up_kernel, parts, (VIR, 8, LANE))
    parts = lax.all_to_all(copies, ("z", "x"), 0, 0, tiled=True)
    return small(finish_kernel, parts, (16, 256))


def solution(mesh):
    grid = Mesh(mesh.devices.reshape(4, 8, 4, 2), ("x", "z", "occ", "rep"))
    vir, group = ("x", "z"), ("occ", "rep")
    return jax.shard_map(
        on_device,
        mesh=grid,
        in_specs=(P(vir, group, None), P(vir, None, group), P()),
        out_specs=P("occ", "rep"),
        check_vma=False,
    )
```

```python
import jax
import jax.numpy as jnp
from jax import lax
from jax.experimental import pallas as pl
from jax.experimental.pallas import tpu as pltpu
from jax.sharding import Mesh
from jax.sharding import PartitionSpec as P

VIR = 32
GRP = 8
BLKS = 8
SLOTS = 12
LANE = 128
AHEAD = 12
MIB = 1 << 20


def spread_kernel(owner_hbm, amp_hbm, slot_ref, out_ref, owner_ref, amp, sems):
    wide = 4 * LANE
    copies = [
        pltpu.make_async_copy(
            amp_hbm.at[:, pl.ds(part * wide, wide)], amp.at[part], sems.at[part]
        )
        for part in range(GRP)
    ]
    owner_copy = pltpu.make_async_copy(owner_hbm, owner_ref, sems.at[GRP])
    owner_copy.start()
    for copy in copies:
        copy.start()

    owner_copy.wait()
    count = owner_ref.shape[1]
    owners = owner_ref[...]
    along = jnp.broadcast_to(owners.astype(jnp.float32), (count, count))
    down = along.T
    rows = lax.broadcasted_iota(jnp.int32, (count, count), 0)
    lanes = lax.broadcasted_iota(jnp.int32, (count, count), 1)
    earlier = jnp.where((down == along) & (rows < lanes), 1, 0)
    rank = jnp.sum(earlier, axis=0, keepdims=True)
    place = lax.rem(owners, 8) * 4 + lax.div(owners, 8)
    slot_ref[...] = place * SLOTS + rank

    for part in range(GRP):
        copies[part].wait()
        for blk in range(BLKS):
            for quarter in range(4):
                first = (quarter * GRP + part) * 8 * BLKS + blk
                out_ref[pl.ds(first, 8, stride=BLKS), :] = amp[
                    part, pl.ds(blk * 8, 8), pl.ds(quarter * LANE, LANE)
                ]


def spread(owners, amp):
    return pl.pallas_call(
        spread_kernel,
        out_shape=[
            jax.ShapeDtypeStruct(owners.shape, jnp.int32),
            jax.ShapeDtypeStruct((VIR * GRP * BLKS, LANE), jnp.float32),
        ],
        in_specs=[pl.BlockSpec(memory_space=pltpu.HBM)] * 2,
        out_specs=[pl.BlockSpec(memory_space=pltpu.VMEM)] * 2,
        scratch_shapes=[
            pltpu.VMEM(owners.shape, jnp.int32),
            pltpu.VMEM((GRP, BLKS * 8, 4 * LANE), jnp.float32),
            pltpu.SemaphoreType.DMA((GRP + 1,)),
        ],
        compiler_params=pltpu.CompilerParams(vmem_limit_bytes=52 * MIB),
        cost_estimate=pl.CostEstimate(flops=0, bytes_accessed=2 * MIB, transcendentals=0),
        name="spread",
    )(owners, amp)


def route_kernel(slot_ref, got_ref, out_ref):
    def clear(i, carry):
        out_ref[pl.ds(i * SLOTS, SLOTS)] = jnp.zeros((SLOTS, GRP, LANE), jnp.float32)
        return carry

    lax.fori_loop(0, VIR, clear, 0)

    for source in range(VIR):
        for blk in range(BLKS):
            x, z = source % 4, source // 4
            vir = x * 8 + z
            out_ref[slot_ref[0, vir * BLKS + blk]] = got_ref[
                pl.ds((x * GRP * 8 + z) * BLKS + blk, GRP, stride=8 * BLKS), :
            ]


def route(slot, got):
    return pl.pallas_call(
        route_kernel,
        out_shape=jax.ShapeDtypeStruct((VIR * SLOTS, GRP, LANE), jnp.float32),
        in_specs=[
            pl.BlockSpec(memory_space=pltpu.SMEM),
            pl.BlockSpec(memory_space=pltpu.VMEM),
        ],
        out_specs=pl.BlockSpec(memory_space=pltpu.VMEM),
        compiler_params=pltpu.CompilerParams(vmem_limit_bytes=8 * MIB),
        cost_estimate=pl.CostEstimate(flops=0, bytes_accessed=3 * MIB, transcendentals=0),
        name="route",
    )(slot, got)


def split(value):
    high = value.astype(jnp.bfloat16)
    return high, (value - high.astype(jnp.float32)).astype(jnp.bfloat16)


def dot_nt(left, right):
    return lax.dot_general(
        left, right, (((1,), (1,)), ((), ())), preferred_element_type=jnp.float32
    )


def contract_kernel(amp_ref, int_hbm, out_ref, held, pair, acc, tiles, sems):
    copies = [
        pltpu.make_async_copy(int_hbm.at[slot], held.at[slot], sems.at[slot])
        for slot in range(SLOTS)
    ]
    for copy in copies[:AHEAD]:
        copy.start()
    acc[...] = jnp.zeros_like(acc)
    for slot in range(SLOTS):
        rows = jnp.concatenate(
            [amp_ref[:, q, slot].reshape(64, LANE) for q in range(4)], axis=1
        )
        pair[slot] = jnp.concatenate(split(rows), axis=0)
    for slot in range(SLOTS):
        copies[slot].wait()
        if slot + AHEAD < SLOTS:
            copies[slot + AHEAD].start()
        b_high, b_low = split(held[slot])
        both = dot_nt(pair[slot], b_high)
        acc[...] += both[:64] + both[64:] + dot_nt(pair[slot, :64], b_low)
    for tile in range(4):
        tiles[tile] = acc[:, pl.ds(tile * LANE, LANE)]
    for piece in range(VIR):
        rep, occ, x = piece // 16, piece // 4 % 4, piece % 4
        out_ref[piece] = tiles[rep * 2 + x % 2, pl.ds(occ * 2 + x // 2, 8, stride=GRP), :]


def contract(amp, integrals):
    return pl.pallas_call(
        contract_kernel,
        out_shape=jax.ShapeDtypeStruct((VIR, 8, LANE), jnp.float32),
        in_specs=[
            pl.BlockSpec(memory_space=pltpu.VMEM),
            pl.BlockSpec(memory_space=pltpu.HBM),
        ],
        out_specs=pl.BlockSpec(memory_space=pltpu.VMEM),
        scratch_shapes=[
            pltpu.VMEM((SLOTS, 512, 512), jnp.float32),
            pltpu.VMEM((SLOTS, 128, 512), jnp.bfloat16),
            pltpu.VMEM((64, 512), jnp.float32),
            pltpu.VMEM((4, 64, LANE), jnp.float32),
            pltpu.SemaphoreType.DMA((SLOTS,)),
        ],
        compiler_params=pltpu.CompilerParams(vmem_limit_bytes=50 * MIB),
        cost_estimate=pl.CostEstimate(
            flops=6 * 64 * 512 * 6144, bytes_accessed=14 * MIB, transcendentals=0
        ),
        name="contract",
    )(amp, integrals)


def add_up_kernel(got_ref, out_ref):
    total = got_ref[0]
    for i in range(1, VIR):
        total = total + got_ref[i]
    for i in range(VIR):
        out_ref[i] = total


def finish_kernel(got_ref, out_ref):
    for x in range(4):
        total = got_ref[x]
        for z in range(1, 8):
            total = total + got_ref[z * 4 + x]
        out_ref[pl.ds(x // 2 * 8, 8), pl.ds(x % 2 * LANE, LANE)] = total


def small(kernel, got, shape):
    return pl.pallas_call(
        kernel,
        out_shape=jax.ShapeDtypeStruct(shape, jnp.float32),
        in_specs=[pl.BlockSpec(memory_space=pltpu.VMEM)],
        out_specs=pl.BlockSpec(memory_space=pltpu.VMEM),
        compiler_params=pltpu.CompilerParams(vmem_limit_bytes=4 * MIB),
        name=kernel.__name__,
    )(got)


def on_device(amplitudes, integrals, block_owner):
    slot, sent = spread(block_owner.reshape(1, -1), amplitudes.reshape(BLKS * 8, 4096))
    sent = sent.reshape(VIR * GRP, BLKS, LANE)
    got = lax.all_to_all(sent, ("x", "occ", "rep", "z"), 0, 0, tiled=True)
    routed = route(slot, got.reshape(VIR * GRP * BLKS, LANE))
    owned = lax.all_to_all(routed.reshape(VIR, SLOTS * GRP, LANE), ("z", "x"), 0, 0, tiled=True)
    pieces = contract(owned.reshape(8, 4, SLOTS, GRP, LANE), integrals)
    parts = lax.all_to_all(pieces, ("rep", "occ", "x"), 0, 0, tiled=True)
    copies = small(add_up_kernel, parts, (VIR, 8, LANE))
    parts = lax.all_to_all(copies, ("z", "x"), 0, 0, tiled=True)
    return small(finish_kernel, parts, (16, 256))


def solution(mesh):
    grid = Mesh(mesh.devices.reshape(4, 8, 4, 2), ("x", "z", "occ", "rep"))
    vir, group = ("x", "z"), ("occ", "rep")
    return jax.shard_map(
        on_device,
        mesh=grid,
        in_specs=(P(vir, group, None), P(vir, None, group), P()),
        out_specs=P("occ", "rep"),
        check_vma=False,
    )
```

```python
import jax
import jax.numpy as jnp
from jax import lax
from jax.experimental import pallas as pl
from jax.experimental.pallas import tpu as pltpu
from jax.sharding import Mesh
from jax.sharding import PartitionSpec as P

VIR = 32
GRP = 8
BLKS = 8
SLOTS = 12
LANE = 128
AHEAD = 12
MIB = 1 << 20


def spread_kernel(amp_hbm, out_ref, amp, sems):
    wide = 4 * LANE
    copies = [
        pltpu.make_async_copy(
            amp_hbm.at[:, pl.ds(part * wide, wide)], amp.at[part], sems.at[part]
        )
        for part in range(GRP)
    ]
    for copy in copies:
        copy.start()

    for part in range(GRP):
        copies[part].wait()
        for blk in range(BLKS):
            for quarter in range(4):
                first = (quarter * GRP + part) * 8 * BLKS + blk
                out_ref[pl.ds(first, 8, stride=BLKS), :] = amp[
                    part, pl.ds(blk * 8, 8), pl.ds(quarter * LANE, LANE)
                ]


def spread(amp):
    return pl.pallas_call(
        spread_kernel,
        out_shape=jax.ShapeDtypeStruct((VIR * GRP * BLKS, LANE), jnp.float32),
        in_specs=[pl.BlockSpec(memory_space=pltpu.HBM)],
        out_specs=pl.BlockSpec(memory_space=pltpu.VMEM),
        scratch_shapes=[
            pltpu.VMEM((GRP, BLKS * 8, 4 * LANE), jnp.float32),
            pltpu.SemaphoreType.DMA((GRP,)),
        ],
        compiler_params=pltpu.CompilerParams(vmem_limit_bytes=52 * MIB),
        cost_estimate=pl.CostEstimate(flops=0, bytes_accessed=2 * MIB, transcendentals=0),
        name="spread",
    )(amp)


def route_kernel(owner_ref, got_ref, out_ref, slots, slot_ref, sem):
    count = owner_ref.shape[1]
    owners = owner_ref[...]
    along = jnp.broadcast_to(owners.astype(jnp.float32), (count, count))
    down = along.T
    rows = lax.broadcasted_iota(jnp.int32, (count, count), 0)
    lanes = lax.broadcasted_iota(jnp.int32, (count, count), 1)
    earlier = jnp.where((down == along) & (rows < lanes), 1, 0)
    rank = jnp.sum(earlier, axis=0, keepdims=True)
    place = lax.rem(owners, 8) * 4 + lax.div(owners, 8)
    slots[...] = place * SLOTS + rank
    to_scalars = pltpu.make_async_copy(slots, slot_ref, sem)
    to_scalars.start()

    def clear(i, carry):
        out_ref[pl.ds(i * SLOTS, SLOTS)] = jnp.zeros((SLOTS, GRP, LANE), jnp.float32)
        return carry

    lax.fori_loop(0, VIR, clear, 0)
    to_scalars.wait()

    for source in range(VIR):
        for blk in range(BLKS):
            x, z = source % 4, source // 4
            vir = x * 8 + z
            out_ref[slot_ref[0, vir * BLKS + blk]] = got_ref[
                pl.ds((x * GRP * 8 + z) * BLKS + blk, GRP, stride=8 * BLKS), :
            ]


def route(owners, got):
    return pl.pallas_call(
        route_kernel,
        out_shape=jax.ShapeDtypeStruct((VIR * SLOTS, GRP, LANE), jnp.float32),
        in_specs=[
            pl.BlockSpec(memory_space=pltpu.VMEM),
            pl.BlockSpec(memory_space=pltpu.VMEM),
        ],
        out_specs=pl.BlockSpec(memory_space=pltpu.VMEM),
        scratch_shapes=[
            pltpu.VMEM(owners.shape, jnp.int32),
            pltpu.SMEM(owners.shape, jnp.int32),
            pltpu.SemaphoreType.DMA,
        ],
        compiler_params=pltpu.CompilerParams(vmem_limit_bytes=8 * MIB),
        cost_estimate=pl.CostEstimate(flops=0, bytes_accessed=3 * MIB, transcendentals=0),
        name="route",
    )(owners, got)


def split(value):
    high = value.astype(jnp.bfloat16)
    return high, (value - high.astype(jnp.float32)).astype(jnp.bfloat16)


def dot_nt(left, right):
    return lax.dot_general(
        left, right, (((1,), (1,)), ((), ())), preferred_element_type=jnp.float32
    )


def contract_kernel(amp_ref, int_hbm, out_ref, held, pair, acc, tiles, sems):
    copies = [
        pltpu.make_async_copy(int_hbm.at[slot], held.at[slot], sems.at[slot])
        for slot in range(SLOTS)
    ]
    for copy in copies[:AHEAD]:
        copy.start()
    acc[...] = jnp.zeros_like(acc)
    for slot in range(SLOTS):
        rows = jnp.concatenate(
            [amp_ref[:, q, slot].reshape(64, LANE) for q in range(4)], axis=1
        )
        pair[slot] = jnp.concatenate(split(rows), axis=0)
    for slot in range(SLOTS):
        copies[slot].wait()
        if slot + AHEAD < SLOTS:
            copies[slot + AHEAD].start()
        b_high, b_low = split(held[slot])
        both = dot_nt(pair[slot], b_high)
        acc[...] += both[:64] + both[64:] + dot_nt(pair[slot, :64], b_low)
    for tile in range(4):
        tiles[tile] = acc[:, pl.ds(tile * LANE, LANE)]
    for piece in range(VIR):
        rep, occ, x = piece // 16, piece // 4 % 4, piece % 4
        out_ref[piece] = tiles[rep * 2 + x % 2, pl.ds(occ * 2 + x // 2, 8, stride=GRP), :]


def contract(amp, integrals):
    return pl.pallas_call(
        contract_kernel,
        out_shape=jax.ShapeDtypeStruct((VIR, 8, LANE), jnp.float32),
        in_specs=[
            pl.BlockSpec(memory_space=pltpu.VMEM),
            pl.BlockSpec(memory_space=pltpu.HBM),
        ],
        out_specs=pl.BlockSpec(memory_space=pltpu.VMEM),
        scratch_shapes=[
            pltpu.VMEM((SLOTS, 512, 512), jnp.float32),
            pltpu.VMEM((SLOTS, 128, 512), jnp.bfloat16),
            pltpu.VMEM((64, 512), jnp.float32),
            pltpu.VMEM((4, 64, LANE), jnp.float32),
            pltpu.SemaphoreType.DMA((SLOTS,)),
        ],
        compiler_params=pltpu.CompilerParams(vmem_limit_bytes=50 * MIB),
        cost_estimate=pl.CostEstimate(
            flops=6 * 64 * 512 * 6144, bytes_accessed=14 * MIB, transcendentals=0
        ),
        name="contract",
    )(amp, integrals)


def add_up_kernel(got_ref, out_ref):
    total = got_ref[0]
    for i in range(1, VIR):
        total = total + got_ref[i]
    for i in range(VIR):
        out_ref[i] = total


def finish_kernel(got_ref, out_ref):
    for x in range(4):
        total = got_ref[x]
        for z in range(1, 8):
            total = total + got_ref[z * 4 + x]
        out_ref[pl.ds(x // 2 * 8, 8), pl.ds(x % 2 * LANE, LANE)] = total


def small(kernel, got, shape):
    return pl.pallas_call(
        kernel,
        out_shape=jax.ShapeDtypeStruct(shape, jnp.float32),
        in_specs=[pl.BlockSpec(memory_space=pltpu.VMEM)],
        out_specs=pl.BlockSpec(memory_space=pltpu.VMEM),
        compiler_params=pltpu.CompilerParams(vmem_limit_bytes=4 * MIB),
        name=kernel.__name__,
    )(got)


def on_device(amplitudes, integrals, block_owner):
    sent = spread(amplitudes.reshape(BLKS * 8, 4096))
    sent = sent.reshape(VIR * GRP, BLKS, LANE)
    got = lax.all_to_all(sent, ("x", "occ", "rep", "z"), 0, 0, tiled=True)
    routed = route(block_owner.reshape(1, -1), got.reshape(VIR * GRP * BLKS, LANE))
    owned = lax.all_to_all(routed.reshape(VIR, SLOTS * GRP, LANE), ("z", "x"), 0, 0, tiled=True)
    pieces = contract(owned.reshape(8, 4, SLOTS, GRP, LANE), integrals)
    parts = lax.all_to_all(pieces, ("rep", "occ", "x"), 0, 0, tiled=True)
    copies = small(add_up_kernel, parts, (VIR, 8, LANE))
    parts = lax.all_to_all(copies, ("z", "x"), 0, 0, tiled=True)
    return small(finish_kernel, parts, (16, 256))


def solution(mesh):
    grid = Mesh(mesh.devices.reshape(4, 8, 4, 2), ("x", "z", "occ", "rep"))
    vir, group = ("x", "z"), ("occ", "rep")
    return jax.shard_map(
        on_device,
        mesh=grid,
        in_specs=(P(vir, group, None), P(vir, None, group), P()),
        out_specs=P("occ", "rep"),
        check_vma=False,
    )
```
